256 devices in a mesh: seq: 32 (over y, z_hi, x), tp: 8 (over z_lo, core).
Axes of the slice: x: 4, y: 4, z: 8 (z_hi: 2, z_lo: 4; z = z_hi * 4 + z_lo), core: 2. Of those that a mesh axis runs over, the one named last changes fastest.
Arguments:
- video_qkv: bfloat16 [8, 32, 2048, 3, 128], P(None, 'tp', 'seq'), may hold values from -110 to 110
- cross_query: bfloat16 [8, 32, 2048, 128], P(None, 'tp', 'seq'), may hold values from -110 to 110
- captions: bfloat16 [8, 192, 4096], P(None, 'tp', 'seq'), may hold values from -700 to 700
- caption_gain: float32 [4096], P('seq'), may hold values from 0.1 to 1.9
- key_value_weight: bfloat16 [4096, 2, 32, 128], P('seq'), may hold values from -0.09375 to 0.09375
- caption_lengths: int32 [8], replicated, may hold values from 1 to 192, 960 in all
Outputs:
- self_out: bfloat16 [8, 32, 2048, 128], P(None, 'tp', 'seq')
- cross_out: bfloat16 [8, 32, 2048, 128], P(None, 'tp', 'seq')
The draws below stay inside these ranges and needn't reach their ends.
Inputs may be any that keep to these rules, and one draw needn't show every extreme that they name: `caption_lengths`: the lengths sum to 960; the longest is exactly 192.
All inputs are finite; a program needn't handle non-finite values.
Results may differ from the reference program's by a relative error of at most 0.012.
The reference program's roundings to bfloat16 on the way count: a program that leaves them out, or rounds other values in their place, can miss the bound.
Values may be sent and summed in bfloat16 or wider, within the bound.
No kernel may reach another device: no remote copies, remote signals or barrier semaphores. Data moves between devices by JAX's collectives and lax.ppermute only.
A program may use at most 64 MiB of HBM per device.

```python
import math
import jax
import jax.numpy as jnp
import numpy as np
from jax import lax

DT = 4096
HEADS = 32
HS = 128
VIDEOS = 8
CAP = 192
LEN = 2048


def draw_video_qkv(key, part):
    key = jax.random.fold_in(key, 11)
    first, second = jax.random.split(key, 2)
    shape = (VIDEOS, HEADS, LEN, 3, HS)
    base = jnp.clip(jax.random.normal(first, shape, jnp.float32), -6.0, 6.0)
    lift = jnp.exp(jax.random.uniform(second, (VIDEOS, HEADS, LEN, 1, 1), jnp.float32, 0.0, math.log(1.5)))
    slot = jnp.arange(3).reshape(1, 1, 1, 3, 1)
    return jnp.clip(jnp.where(slot == 0, base * lift, base), -110.0, 110.0).astype(jnp.bfloat16)


def draw_cross_query(key, part):
    key = jax.random.fold_in(key, 12)
    first, second = jax.random.split(key, 2)
    shape = (VIDEOS, HEADS, LEN, HS)
    base = jnp.clip(jax.random.normal(first, shape, jnp.float32), -6.0, 6.0)
    lift = jnp.exp(jax.random.uniform(second, (VIDEOS, HEADS, LEN, 1), jnp.float32, 0.0, math.log(1.5)))
    return jnp.clip(base * lift, -110.0, 110.0).astype(jnp.bfloat16)


def draw_captions(key, part):
    key = jax.random.fold_in(key, 13)
    first, second, third = jax.random.split(key, 3)
    columns = jnp.arange(DT, dtype=jnp.float32)
    rising = jnp.exp(math.log(3.0) * columns / DT)
    base = jnp.clip(jax.random.normal(first, (VIDEOS, CAP, DT), jnp.float32), -6.0, 6.0)
    row_scale = jnp.exp(jax.random.uniform(second, (VIDEOS, CAP, 1), jnp.float32, 0.0, math.log(10.0)))
    column_scale = jnp.exp(jax.random.uniform(third, (1, 1, DT), jnp.float32, 0.0, math.log(3.0)))
    return jnp.clip(base * row_scale * rising * column_scale, -700.0, 700.0).astype(jnp.bfloat16)


def block_scale(rng, shape, pieces, low, largest):
    loudness, own = 1.0, jax.random.fold_in(rng, 6)
    for axis_at, blocks in pieces:
        heights = jnp.exp(jax.random.uniform(jax.random.fold_in(own, axis_at), (blocks,), jnp.float32, low / len(pieces), largest / len(pieces)))
        loudness = loudness * jnp.repeat(heights, shape[axis_at] // blocks).reshape([-1 if axis == axis_at else 1 for axis in range(len(shape))])
    return loudness


def split_up(count, total, most, skew):
    portions = [(1 << 20) // math.isqrt(grade ** skew) + 1 for grade in range(2, count + 1)]
    spare, counts = total - most - (count - 1), [1] * (count - 1)
    while spare > 0:
        candidates = [i for i in range(count - 1) if counts[i] < most]
        whole, budget = sum([portions[i] for i in candidates]), spare
        for i in candidates:
            extra = min(most - counts[i], max(1, budget * portions[i] // whole), spare)
            counts[i] = counts[i] + extra
            spare = spare - extra
    return np.array([most] + counts)


def uneven_parts(own_key, amount, total, reach, slope):
    if amount == 2:
        one = jax.random.randint(own_key, (), max(1, total - reach), min(reach, total - 1) + 1)
        return jnp.stack([one, total - one])
    tallies = jnp.asarray(split_up(amount, total, reach, slope), jnp.int32)
    pairs = (amount - 1) // 2
    source_of, sink = tallies[1:1 + 2 * pairs:2], tallies[2:2 + 2 * pairs:2]
    slack = jnp.minimum(source_of - 1, reach - sink)
    moved = jax.random.randint(jax.random.fold_in(own_key, 1), (pairs,), 0, 1 << 20) % (slack + 1)
    tallies = tallies.at[1:1 + 2 * pairs:2].set(source_of - moved).at[2:2 + 2 * pairs:2].set(sink + moved)
    return tallies[jax.random.permutation(jax.random.fold_in(own_key, 2), amount)]


def gaussian(key, shape, spread, bound, pieces=(), held_as=jnp.bfloat16):
    result = spread * jax.random.normal(key, shape, jnp.float32)
    if pieces:
        result = result * block_scale(key, shape, pieces, -0.22, 0.18)
    return jnp.clip(result, -bound, bound).astype(held_as)


def setup_inputs(seed: int = 0) -> dict:
    arg_keys = jax.random.split(jax.random.key(seed), 7)
    video_qkv = draw_video_qkv(jax.random.fold_in(arg_keys[6], 71), 0)
    cross_query = draw_cross_query(jax.random.fold_in(arg_keys[6], 71), 0)
    captions = draw_captions(jax.random.fold_in(arg_keys[6], 71), 0)
    caption_gain = jnp.clip(1.0 + 0.18 * jax.random.normal(arg_keys[3], (DT,), jnp.float32), 0.1, 1.9)
    key_value_weight = gaussian(arg_keys[4], (DT, 2, HEADS, HS), DT ** -0.5, 0.09375, ((0, 32),))
    caption_lengths = uneven_parts(arg_keys[5], VIDEOS, 5 * CAP, CAP, 1).astype(jnp.int32)
    return {"video_qkv": video_qkv, "cross_query": cross_query, "captions": captions, "caption_gain": caption_gain, "key_value_weight": key_value_weight, "caption_lengths": caption_lengths}


norm_eps = 1e-06
masked_score = -1e+30

def attend(queries, key_rows, value_rows, allowed):
    scores = jnp.dot(queries, key_rows.T, preferred_element_type=jnp.float32) * queries.shape[-1] ** (-0.5)
    scores = jnp.where(allowed, scores, masked_score)
    row_top = lax.optimization_barrier(jnp.max(scores, axis=-1, keepdims=True))
    lifted = jnp.exp(scores - row_top)
    weights = (lifted / lax.optimization_barrier(jnp.sum(lifted, axis=-1, keepdims=True))).astype(jnp.bfloat16)
    return jnp.dot(weights, value_rows, preferred_element_type=jnp.float32).astype(jnp.bfloat16)

def reference(video_qkv, cross_query, captions, caption_gain, key_value_weight, caption_lengths):
    widened = captions.astype(jnp.float32)
    squares = lax.optimization_barrier(jnp.sum(widened * widened, axis=-1))
    inverse = lax.rsqrt(squares / DT + norm_eps)
    scaled = (widened * caption_gain).astype(jnp.bfloat16)
    projected = jnp.dot(scaled.reshape(VIDEOS * CAP, DT), key_value_weight.reshape(DT, 2 * HEADS * HS), preferred_element_type=jnp.float32)
    caption_kv = (projected * inverse.reshape(VIDEOS * CAP, 1)).astype(jnp.bfloat16)
    caption_kv = caption_kv.reshape(VIDEOS, CAP, 2, HEADS, HS).transpose(0, 3, 2, 1, 4)
    caption_kv = caption_kv.reshape(VIDEOS * HEADS, 2, CAP, HS)
    work_items = video_qkv.reshape(VIDEOS * HEADS, LEN, 3, HS)

    def self_item(one_item):
        return attend(one_item[:, 0], one_item[:, 1], one_item[:, 2], True)
    self_out = lax.map(self_item, work_items).reshape(VIDEOS, HEADS, LEN, HS)
    positions = jnp.arange(CAP, dtype=jnp.int32)
    allowed = positions[None, :] < caption_lengths[:, None]
    allowed = jnp.repeat(allowed, HEADS, axis=0)
    queries = cross_query.reshape(VIDEOS * HEADS, LEN, HS)

    def cross_item(packed):
        item_queries, item_kv, item_allowed = packed
        return attend(item_queries, item_kv[0], item_kv[1], item_allowed[None, :])
    cross_out = lax.map(cross_item, (queries, caption_kv, allowed)).reshape(VIDEOS, HEADS, LEN, HS)
    return (self_out, cross_out)
```

```python
import jax
import jax.numpy as jnp
from jax import lax
from jax.experimental import pallas as pl
from jax.experimental.pallas import tpu as pltpu
from jax.sharding import Mesh
from jax.sharding import PartitionSpec as P

norm_eps = 1e-06
masked_score = -1e30
log2e = 1.4426950408889634
AXES = ("y", "zh", "x", "zl", "c")
SEQ = ("y", "zh", "x")
XY = ("y", "x")
TP = ("zl", "c")
SWAP = [(0, 1), (1, 0)]
VMEM_LIMIT = 40 * 1024 * 1024


def nt_dot(a, b):
    return lax.dot_general(a, b, (((1,), (1,)), ((), ())), preferred_element_type=jnp.float32)


def softmax_dot(scores, values, scale):
    top = jnp.max(scores, axis=-1, keepdims=True)
    lifted = jnp.exp2((scores - top) * (scale * log2e))
    total = jnp.sum(lifted, axis=-1, keepdims=True)
    out = jnp.dot(lifted.astype(jnp.bfloat16), values, preferred_element_type=jnp.float32)
    return (out / total).astype(jnp.bfloat16)


def self_kernel(q_ref, kv_ref, o_ref):
    head_size = o_ref.shape[-1]
    scores = nt_dot(q_ref[:, :head_size], kv_ref[:, head_size : 2 * head_size])
    o_ref[...] = softmax_dot(scores, kv_ref[:, 2 * head_size :], head_size ** (-0.5))


def self_attention(item, block=256):
    full_len, width = item.shape
    head_size = width // 3
    return pl.pallas_call(
        self_kernel,
        out_shape=jax.ShapeDtypeStruct((full_len, head_size), item.dtype),
        grid=(full_len // block,),
        in_specs=[
            pl.BlockSpec((block, width), lambda i: (i, 0)),
            pl.BlockSpec((full_len, width), lambda i: (0, 0)),
        ],
        out_specs=pl.BlockSpec((block, head_size), lambda i: (i, 0)),
        compiler_params=pltpu.CompilerParams(vmem_limit_bytes=VMEM_LIMIT),
        cost_estimate=pl.CostEstimate(
            flops=4 * full_len * full_len * head_size,
            bytes_accessed=8 * full_len * head_size,
            transcendentals=full_len * full_len,
        ),
        name="self_attention",
    )(item, item)


def project_kernel(mine_ref, other_ref, w_ref, part_ref, sq_ref):
    z_count, sources, rows, feats = mine_ref.shape
    half = z_count * rows
    for which, ref in enumerate((mine_ref, other_ref)):
        squares = jnp.zeros((half, 1), jnp.float32)
        total = jnp.zeros((half, part_ref.shape[1]), jnp.float32)
        for s in range(sources):
            block = ref[:, s].astype(jnp.float32).reshape(half, feats)
            squares += jnp.sum(block * block, axis=-1, keepdims=True)
            gains = w_ref[s, feats : feats + 16, :feats].astype(jnp.float32)
            gain = gains[0:1] + gains[1:2] + gains[2:3]
            scaled = (block * gain).astype(jnp.bfloat16)
            total += jnp.dot(scaled, w_ref[s, :feats], preferred_element_type=jnp.float32)
        part_ref[which * half : (which + 1) * half] = total
        spread = jnp.broadcast_to(squares, (half, 128))
        sq_ref[which] = spread.T[:8]


def project(mine, other, weights):
    z_count, sources, rows, feats = mine.shape
    half = z_count * rows
    return pl.pallas_call(
        project_kernel,
        out_shape=(
            jax.ShapeDtypeStruct((2 * half, weights.shape[-1]), jnp.float32),
            jax.ShapeDtypeStruct((2, 8, half), jnp.float32),
        ),
        compiler_params=pltpu.CompilerParams(vmem_limit_bytes=VMEM_LIMIT),
        cost_estimate=pl.CostEstimate(
            flops=4 * half * sources * feats * weights.shape[-1],
            bytes_accessed=4 * half * sources * feats,
            transcendentals=0,
        ),
        name="project",
    )(mine, other, weights)


def cross_kernel(full_width, q_ref, part_a, part_b, sq_a, sq_b, allowed_ref, o_ref):
    sources, videos, local_len, head_size = q_ref.shape
    half = sq_a.shape[-1]
    blocks, rows = 8, part_a.shape[0] // 8
    per = rows // videos
    inverse = []
    for which in range(2):
        squares = sq_a[which, 0:1] + sq_b[which, 0:1]
        inv = lax.rsqrt(squares / full_width + norm_eps)
        inverse.append(jnp.broadcast_to(inv, (128, half)).T)
    kv = []
    for b in range(blocks):
        span = slice(b * rows, (b + 1) * rows)
        total = part_a[span] + part_b[span]
        at = (b % 4) * rows
        inv = inverse[b // 4][at : at + rows]
        kv.append(jnp.concatenate([total[:, :head_size] * inv, total[:, head_size:] * inv], axis=1))
    for v in range(videos):
        this = jnp.concatenate([blk[v * per : (v + 1) * per] for blk in kv], axis=0)
        this = this.astype(jnp.bfloat16)
        queries = q_ref[:, v].reshape(sources * local_len, head_size)
        scores = nt_dot(queries, this[:, :head_size])
        scores = jnp.where(allowed_ref[v, 0:1] > 0, scores, masked_score)
        out = softmax_dot(scores, this[:, head_size:], head_size ** (-0.5))
        o_ref[:, v] = out.reshape(sources, local_len, head_size)


def cross_attention(queries, part_a, part_b, sq_a, sq_b, allowed, full_width):
    sources, videos, local_len, head_size = queries.shape
    count = sources * videos * local_len * allowed.shape[-1]

    def kernel(*refs):
        cross_kernel(full_width, *refs)

    return pl.pallas_call(
        kernel,
        out_shape=jax.ShapeDtypeStruct(queries.shape, queries.dtype),
        compiler_params=pltpu.CompilerParams(vmem_limit_bytes=VMEM_LIMIT),
        cost_estimate=pl.CostEstimate(
            flops=4 * count * head_size,
            bytes_accessed=4 * sources * videos * local_len * head_size,
            transcendentals=count,
        ),
        name="cross_attention",
    )(queries, part_a, part_b, sq_a, sq_b, allowed)


def three_parts(values):
    high = lax.reduce_precision(values, 8, 7)
    rest = values - high
    middle = lax.reduce_precision(rest, 8, 7)
    return [p.astype(jnp.bfloat16) for p in (high, middle, rest - middle)]


def body(video_qkv, cross_query, captions, caption_gain, key_value_weight, caption_lengths):
    videos, local_heads, local_len, slots, head_size = video_qkv.shape
    caption_len, feats = captions.shape[1:]
    ny, nx, nz = lax.axis_size("y"), lax.axis_size("x"), lax.axis_size("zl")
    pair = videos // ny
    group = ny * nx
    tp = lax.axis_index("zl") * 2 + lax.axis_index("c")
    full_width = feats * group * 2

    rows = captions.reshape(ny, 1, pair * caption_len, feats)
    rows = jnp.broadcast_to(rows, (ny, nx, pair * caption_len, feats))
    rows = rows.reshape(group, pair * caption_len, feats)
    rows = lax.all_to_all(rows, XY, split_axis=0, concat_axis=0, tiled=True)
    rows = lax.all_gather(rows, "zl", axis=0, tiled=False)
    other_rows = lax.ppermute(rows, "c", SWAP)

    weights = lax.dynamic_slice_in_dim(key_value_weight, tp * local_heads, local_heads, axis=2)
    weights = weights.transpose(2, 0, 1, 3).reshape(local_heads, feats, 2 * head_size)
    gains = jnp.stack(three_parts(caption_gain))
    gains = jnp.pad(gains, ((0, 13), (0, 2 * head_size - feats)))
    gains = jnp.broadcast_to(gains, (local_heads,) + gains.shape)
    weights = jnp.concatenate([weights, gains], axis=1)
    weights = jnp.broadcast_to(weights, (ny,) + weights.shape).reshape(
        (group,) + weights.shape[1:]
    )
    weights = lax.all_to_all(weights, XY, split_axis=0, concat_axis=0, tiled=True)

    items = video_qkv.reshape(videos * local_heads, local_len, slots * head_size)
    items = lax.all_to_all(items, SEQ, split_axis=0, concat_axis=0, tiled=True)

    queries = cross_query.reshape(ny, pair, nx, local_len, head_size).transpose(0, 2, 1, 3, 4)
    queries = queries.reshape(group, pair, local_len, head_size)
    queries = lax.all_to_all(queries, XY, split_axis=0, concat_axis=0, tiled=True)

    part, squares = project(rows, other_rows, weights)
    far_part = lax.ppermute(part, "zh", SWAP)
    far_squares = lax.ppermute(squares, "zh", SWAP)

    attended = self_attention(items.reshape(-1, slots * head_size))
    attended = attended.reshape(videos * local_heads, local_len, head_size)
    self_out = lax.all_to_all(attended, SEQ, split_axis=0, concat_axis=0, tiled=True)
    self_out = self_out.reshape(videos, local_heads, local_len, head_size)

    core = lax.axis_index("c")
    which, z, token = jnp.meshgrid(
        jnp.arange(2), jnp.arange(nz), jnp.arange(caption_len), indexing="ij"
    )
    cores = jnp.where(which == 0, core, 1 - core)
    positions = ((z * 2 + cores) * caption_len + token).reshape(-1)
    lengths = lax.dynamic_slice_in_dim(caption_lengths, lax.axis_index("y") * pair, pair)
    allowed = (positions[None, :] < lengths[:, None]).astype(jnp.float32)
    allowed = jnp.broadcast_to(allowed[:, None, :], (pair, 8, allowed.shape[-1]))

    crossed = cross_attention(queries, part, far_part, squares, far_squares, allowed, full_width)
    crossed = lax.all_to_all(crossed, XY, split_axis=0, concat_axis=0, tiled=True)
    crossed = crossed.reshape(ny, nx, pair, local_len, head_size).transpose(0, 2, 1, 3, 4)
    cross_out = crossed.reshape(videos, local_heads, local_len, head_size)
    return (self_out, cross_out)


def solution(mesh):
    devices = mesh.devices.reshape(4, 2, 4, 4, 2)
    placed = (
        P(None, TP, SEQ, None, None),
        P(None, TP, SEQ, None),
        P(None, TP, SEQ),
        P(SEQ),
        P(SEQ, None, None, None),
        P(),
    )
    return jax.shard_map(
        body,
        mesh=Mesh(devices, AXES),
        in_specs=placed,
        out_specs=(P(None, TP, SEQ, None), P(None, TP, SEQ, None)),
        check_vma=False,
    )
```

```python
import jax
import jax.numpy as jnp
from jax import lax
from jax.experimental import pallas as pl
from jax.experimental.pallas import tpu as pltpu
from jax.sharding import Mesh
from jax.sharding import PartitionSpec as P

norm_eps = 1e-06
masked_score = -1e30
log2e = 1.4426950408889634
AXES = ("y", "zh", "x", "zl", "c")
SEQ = ("y", "zh", "x")
XY = ("y", "x")
TP = ("zl", "c")
SWAP = [(0, 1), (1, 0)]
PLACE_FLOPS = 100_000_000_000
VMEM_LIMIT = 40 * 1024 * 1024


def nt_dot(a, b):
    return lax.dot_general(a, b, (((1,), (1,)), ((), ())), preferred_element_type=jnp.float32)


def softmax_dot(scores, values, scale):
    top = jnp.max(scores, axis=-1, keepdims=True)
    lifted = jnp.exp2((scores - top) * (scale * log2e))
    total = jnp.sum(lifted, axis=-1, keepdims=True)
    out = jnp.dot(lifted.astype(jnp.bfloat16), values, preferred_element_type=jnp.float32)
    return (out / total).astype(jnp.bfloat16)


def params():
    return pltpu.CompilerParams(vmem_limit_bytes=VMEM_LIMIT)


def whole(array):
    return pl.BlockSpec(array.shape, lambda *_: (0,) * array.ndim)


def pick_kernel(zh_ref, x_ref, o_ref):
    o_ref[...] = x_ref[...].reshape(o_ref.shape)


def pick(zh, items):
    ny, _, nx, height, lanes = items.shape
    return pl.pallas_call(
        pick_kernel,
        out_shape=jax.ShapeDtypeStruct((ny * nx, height, lanes), items.dtype),
        grid_spec=pltpu.PrefetchScalarGridSpec(
            num_scalar_prefetch=1,
            grid=(2,),
            in_specs=[
                pl.BlockSpec(
                    (ny // 2, 1, nx, height, lanes), lambda i, zh_ref: (i, zh_ref[0], 0, 0, 0)
                )
            ],
            out_specs=pl.BlockSpec((ny // 2 * nx, height, lanes), lambda i, zh_ref: (i, 0, 0)),
        ),
        name="pick",
    )(zh, items)


def pack_kernel(zh_ref, x_ref, q_ref, *refs):
    o_ref = refs[-1]
    ny, _, nx, height, lanes = x_ref.shape
    pair, local_len = q_ref.shape[1], q_ref.shape[3]
    o_ref[:, :height] = x_ref[...].reshape(ny * nx, height, lanes)
    for y in range(ny):
        for j in range(pair):
            at = 2 * height + j * local_len
            o_ref[y * nx : (y + 1) * nx, at : at + local_len] = q_ref[y, j]


def pack(zh, items, queries, earlier):
    ny, _, nx, height, lanes = items.shape
    pair, local_len = queries.shape[1], queries.shape[3]
    total = 2 * height + pair * local_len
    return pl.pallas_call(
        pack_kernel,
        out_shape=jax.ShapeDtypeStruct((ny * nx, total, lanes), items.dtype),
        grid_spec=pltpu.PrefetchScalarGridSpec(
            num_scalar_prefetch=1,
            grid=(2,),
            in_specs=[
                pl.BlockSpec(
                    (ny // 2, 1, nx, height, lanes), lambda i, zh_ref: (i, zh_ref[0], 0, 0, 0)
                ),
                pl.BlockSpec(
                    (ny // 2, pair, nx, local_len, lanes), lambda i, zh_ref: (i, 0, 0, 0, 0)
                ),
            ]
            + [pl.BlockSpec(memory_space=pl.ANY)] * len(earlier),
            out_specs=pl.BlockSpec((ny // 2 * nx, total, lanes), lambda i, zh_ref: (i, 0, 0)),
        ),
        name="pack",
    )(zh, items, queries, *earlier)


def place_kernel(x_ref, _, o_ref):
    o_ref[...] = x_ref[...]


def place(buffer, part, at):
    count, height, lanes = part.shape
    return pl.pallas_call(
        place_kernel,
        out_shape=jax.ShapeDtypeStruct(buffer.shape, buffer.dtype),
        grid=(2,),
        in_specs=[
            pl.BlockSpec((count // 2, height, lanes), lambda i: (i, 0, 0)),
            pl.BlockSpec(memory_space=pl.ANY),
        ],
        out_specs=pl.BlockSpec((count // 2, height, lanes), lambda i: (i, at, 0)),
        input_output_aliases={1: 0},
        cost_estimate=pl.CostEstimate(
            flops=PLACE_FLOPS, bytes_accessed=4 * part.size, transcendentals=0
        ),
        name="place",
    )(part, buffer)


def take_kernel(x_ref, *refs):
    refs[-1][...] = x_ref[...]


def take(buffer, height, earlier):
    count, _, lanes = buffer.shape
    block = pl.BlockSpec((count // 2, height, lanes), lambda i: (i, 0, 0))
    return pl.pallas_call(
        take_kernel,
        out_shape=jax.ShapeDtypeStruct((count, height, lanes), buffer.dtype),
        grid=(2,),
        in_specs=[block] + [pl.BlockSpec(memory_space=pl.ANY)] * len(earlier),
        out_specs=block,
        name="take",
    )(buffer, *earlier)


def self_kernel(from_far, x_ref, *refs):
    o_ref = refs[-1]
    sources, local_len, head_size = o_ref.shape
    count = sources * local_len
    scale = head_size ** (-0.5) * log2e

    def slot(k):
        return x_ref[:, k * local_len : (k + 1) * local_len].reshape(count, head_size)

    ones = jnp.ones((count, head_size), jnp.bfloat16)
    keys = [slot(1), slot(4)]
    values = [jnp.concatenate([slot(k), ones], axis=1) for k in (2, 5)]
    queries = slot(3 * from_far)
    block = 2
    for at in range(0, sources, block):
        some = queries[at * local_len : (at + block) * local_len]
        scores = [nt_dot(some, k) for k in keys]
        top = jnp.maximum(*(jnp.max(s, axis=-1, keepdims=True) for s in scores))
        lifted = [jnp.exp2((s - top) * scale).astype(jnp.bfloat16) for s in scores]
        sums = [
            jnp.dot(l, v, preferred_element_type=jnp.float32) for l, v in zip(lifted, values)
        ]
        sums = sums[0] + sums[1]
        out = (sums[:, :head_size] / sums[:, head_size:]).astype(jnp.bfloat16)
        o_ref[at : at + block] = out.reshape(block, local_len, head_size)


def self_attention(packed, from_far, height, room, earlier):
    sources, _, head_size = packed.shape
    local_len = height // 3
    full_len = 2 * sources * local_len

    def kernel(*refs):
        self_kernel(from_far, *refs)

    return pl.pallas_call(
        kernel,
        out_shape=jax.ShapeDtypeStruct((sources, room, head_size), packed.dtype),
        grid=(1,),
        in_specs=[pl.BlockSpec((sources, 2 * height, head_size), lambda i: (0, 0, 0))]
        + [pl.BlockSpec(memory_space=pl.ANY)] * len(earlier),
        out_specs=pl.BlockSpec(
            (sources, local_len, head_size), lambda i: (0, room // local_len - 1, 0)
        ),
        compiler_params=params(),
        cost_estimate=pl.CostEstimate(
            flops=2 * full_len * full_len * head_size,
            bytes_accessed=6 * full_len * head_size,
            transcendentals=full_len * full_len // 2,
        ),
        name="self_attention",
    )(packed, *earlier)


def project_kernel(got_ref, other_ref, part_ref):
    sources, taken, feats = other_ref.shape
    head_size = part_ref.shape[-1] // 2
    per = 48
    blocks = taken // per
    for which, ref in enumerate((got_ref, other_ref)):
        squares = jnp.zeros((taken, 1), jnp.float32)
        total = [jnp.zeros((taken, head_size), jnp.float32) for _ in range(2)]
        for s in range(sources):
            block = ref[s, :taken].astype(jnp.float32)
            squares += jnp.sum(block * block, axis=-1, keepdims=True)
            after = taken + 2 * feats
            parts = got_ref[s, after : after + 16].astype(jnp.float32)
            gain = parts[0:1] + parts[1:2] + parts[2:3]
            scaled = (block * gain).astype(jnp.bfloat16)
            for k in range(2):
                at = taken + k * feats
                total[k] += jnp.dot(
                    scaled, got_ref[s, at : at + feats], preferred_element_type=jnp.float32
                )
        both = jnp.concatenate(total, axis=1)
        part_ref[which * taken : (which + 1) * taken] = both
        spread = jnp.broadcast_to(squares, (taken, 128)).T[:8]
        spread = jnp.concatenate([spread, jnp.zeros((8, 2 * head_size - taken))], axis=1)
        at = 2 * taken + 8 * which
        part_ref[at : at + 8] = spread


def project(got, other, head_size):
    sources, taken, feats = other.shape
    return pl.pallas_call(
        project_kernel,
        out_shape=jax.ShapeDtypeStruct((2 * taken + 16, 2 * head_size), jnp.float32),
        compiler_params=params(),
        cost_estimate=pl.CostEstimate(
            flops=8 * taken * sources * feats * head_size,
            bytes_accessed=4 * got.size,
            transcendentals=0,
        ),
        name="project",
    )(got, other)


def cross_kernel(full_width, q_ref, part_a, part_b, allowed_ref, far_ref, _, o_ref):
    sources, height, head_size = q_ref.shape
    videos = allowed_ref.shape[0]
    local_len = height // videos
    o_ref[:, height:] = far_ref[...]
    half = part_a.shape[0] // 2 - 8
    blocks, rows = 8, half // 4
    per = rows // videos
    inverse = []
    for which in range(2):
        at = 2 * half + 8 * which
        squares = part_a[at : at + 1, :half] + part_b[at : at + 1, :half]
        inv = lax.rsqrt(squares / full_width + norm_eps)
        inverse.append(jnp.broadcast_to(inv, (128, half)).T)
    kv = []
    for b in range(blocks):
        span = slice(b * rows, (b + 1) * rows)
        total = part_a[span] + part_b[span]
        at = (b % 4) * rows
        inv = inverse[b // 4][at : at + rows]
        kv.append(jnp.concatenate([total[:, :head_size] * inv, total[:, head_size:] * inv], axis=1))
    for v in range(videos):
        this = jnp.concatenate([blk[v * per : (v + 1) * per] for blk in kv], axis=0)
        this = this.astype(jnp.bfloat16)
        rows_of_v = slice(v * local_len, (v + 1) * local_len)
        for at in range(0, sources, 4):
            queries = q_ref[at : at + 4, rows_of_v].reshape(4 * local_len, head_size)
            scores = nt_dot(queries, this[:, :head_size])
            scores = jnp.where(allowed_ref[v, 0:1] > 0, scores, masked_score)
            out = softmax_dot(scores, this[:, head_size:], head_size ** (-0.5))
            o_ref[at : at + 4, rows_of_v] = out.reshape(4, local_len, head_size)


def cross_attention(packed, part, far_part, allowed, far_out, outs, height, full_width):
    sources, total, head_size = packed.shape
    taken = total - 2 * height
    count = sources * taken * allowed.shape[-1]

    def kernel(*refs):
        cross_kernel(full_width, *refs)

    return pl.pallas_call(
        kernel,
        out_shape=jax.ShapeDtypeStruct(outs.shape, outs.dtype),
        grid=(1,),
        in_specs=[pl.BlockSpec((sources, taken, head_size), lambda i: (0, 2 * height // taken, 0))]
        + [whole(one) for one in (part, far_part, allowed, far_out)]
        + [pl.BlockSpec(memory_space=pl.ANY)],
        out_specs=pl.BlockSpec(
            (sources, taken + far_out.shape[1], head_size), lambda i: (0, 0, 0)
        ),
        input_output_aliases={5: 0},
        compiler_params=params(),
        cost_estimate=pl.CostEstimate(
            flops=4 * count * head_size,
            bytes_accessed=4 * sources * taken * head_size,
            transcendentals=count,
        ),
        name="cross_attention",
    )(packed, part, far_part, allowed, far_out, outs)


def unpack_kernel(zh_ref, x_ref, self_ref, cross_ref):
    ny, pair, nx, local_len, head_size = self_ref.shape
    got = x_ref[...].reshape(ny, nx, 2 * pair * local_len, head_size)
    zh = zh_ref[0]
    for y in range(ny):
        for j in range(pair):
            cross_ref[y, j] = got[y, :, j * local_len : (j + 1) * local_len]
        self_ref[y, 1 - zh] = got[y, :, pair * local_len : (pair + 1) * local_len]
        self_ref[y, zh] = got[y, :, (pair + 1) * local_len :]


def unpack(zh, got, shape):
    ny, pair, nx, local_len, head_size = shape
    out = pl.BlockSpec((ny // 2,) + shape[1:], lambda i: (i, 0, 0, 0, 0))
    return pl.pallas_call(
        unpack_kernel,
        out_shape=(jax.ShapeDtypeStruct(shape, got.dtype),) * 2,
        grid=(2,),
        in_specs=[
            pl.BlockSpec(memory_space=pltpu.SMEM),
            pl.BlockSpec((ny // 2 * nx,) + got.shape[1:], lambda i: (i, 0, 0)),
        ],
        out_specs=(out, out),
        name="unpack",
    )(zh, got)


def hold_kernel(*refs):
    pass


def hold(value, earlier):
    return pl.pallas_call(
        hold_kernel,
        out_shape=jax.ShapeDtypeStruct(value.shape, value.dtype),
        in_specs=[pl.BlockSpec(memory_space=pl.ANY)] * (1 + len(earlier)),
        out_specs=pl.BlockSpec(memory_space=pl.ANY),
        input_output_aliases={0: 0},
        name="hold",
    )(value, *earlier)


def three_parts(values):
    high = lax.reduce_precision(values, 8, 7)
    rest = values - high
    middle = lax.reduce_precision(rest, 8, 7)
    return [p.astype(jnp.bfloat16) for p in (high, middle, rest - middle)]


def ahead(value, axis, step):
    return lax.ppermute(value, axis, [(i, (i + step) % 4) for i in range(4)])


def gather_ring(value, axis):
    return [value] + [ahead(value, axis, k) for k in (1, 3, 2)]


def ring_order(pieces):
    own, one, three, two = pieces
    return [own, one, two, three]


def body(video_qkv, cross_query, captions, caption_gain, key_value_weight, caption_lengths):
    videos, local_heads, local_len, slots, head_size = video_qkv.shape
    caption_len, feats = captions.shape[1:]
    ny, nx, nz = lax.axis_size("y"), lax.axis_size("x"), lax.axis_size("zl")
    pair, group, height = videos // ny, ny * nx, slots * local_len
    at_y, at_z, core = (lax.axis_index(a) for a in ("y", "zl", "c"))
    zh = lax.axis_index("zh").astype(jnp.int32).reshape(1)
    full_width = feats * group * 2

    items = video_qkv.transpose(0, 1, 3, 2, 4)
    items = items.reshape(ny, pair, nx, height, head_size)
    rows = ring_order(gather_ring(captions, "zl"))
    far = lax.ppermute(hold(pick(1 - zh, items), rows[1:]), "zh", SWAP)
    rows = jnp.stack(rows)
    rows = rows.reshape(nz, ny, pair * caption_len, feats).transpose(1, 0, 2, 3)
    taken = nz * pair * caption_len
    rows = rows.reshape(ny, 1, taken, feats)
    first = (at_z * 2 + core) * local_heads
    weights = lax.dynamic_slice_in_dim(key_value_weight, first, local_heads, axis=2)
    weights = weights.transpose(2, 1, 0, 3).reshape(1, nx, 2 * feats, head_size)
    gains = jnp.pad(jnp.stack(three_parts(caption_gain)), ((0, 13), (0, 0)))
    sent = jnp.concatenate(
        [
            jnp.broadcast_to(rows, (ny, nx, taken, feats)),
            jnp.broadcast_to(weights, (ny, nx, 2 * feats, head_size)),
            jnp.broadcast_to(gains, (ny, nx, 16, feats)),
        ],
        axis=2,
    ).reshape(group, taken + 2 * feats + 16, feats)
    got = lax.all_to_all(sent, XY, split_axis=0, concat_axis=0, tiled=True)
    queries = cross_query.reshape(ny, pair, nx, local_len, head_size)
    packed = hold(place(pack(zh, items, queries, []), far, 1), [got])
    other = lax.ppermute(take(got, taken, [packed]), "c", SWAP)
    part = project(got, other, head_size)
    far_part = lax.ppermute(part, "zh", SWAP)

    packed = lax.all_to_all(packed, XY, split_axis=0, concat_axis=0, tiled=True)

    far_out = self_attention(packed, 1, height, local_len, [part])
    far_out = lax.ppermute(far_out, "zh", SWAP)
    outs = self_attention(packed, 0, height, 2 * pair * local_len, [])

    which, z, token = jnp.meshgrid(
        jnp.arange(2), jnp.arange(nz), jnp.arange(caption_len), indexing="ij"
    )
    cores = jnp.where(which == 0, core, 1 - core)
    positions = (((at_z + nz - z) % nz * 2 + cores) * caption_len + token).reshape(-1)
    lengths = lax.dynamic_slice_in_dim(caption_lengths, at_y * pair, pair)
    allowed = (positions[None, :] < lengths[:, None]).astype(jnp.float32)
    allowed = jnp.broadcast_to(allowed[:, None, :], (pair, 8, allowed.shape[-1]))
    outs = cross_attention(packed, part, far_part, allowed, far_out, outs, height, full_width)
    outs = lax.all_to_all(outs, XY, split_axis=0, concat_axis=0, tiled=True)
    self_out, cross_out = unpack(zh, outs, (ny, pair, nx, local_len, head_size))
    shape = (videos, local_heads, local_len, head_size)
    return (self_out.reshape(shape), cross_out.reshape(shape))


def solution(mesh):
    devices = mesh.devices.reshape(4, 2, 4, 4, 2)
    placed = (
        P(None, TP, SEQ, None, None),
        P(None, TP, SEQ, None),
        P(None, TP, SEQ),
        P(SEQ),
        P(SEQ, None, None, None),
        P(),
    )
    return jax.shard_map(
        body,
        mesh=Mesh(devices, AXES),
        in_specs=placed,
        out_specs=(P(None, TP, SEQ, None), P(None, TP, SEQ, None)),
        check_vma=False,
    )
```

```python
import jax
import jax.numpy as jnp
from jax import lax
from jax.experimental import pallas as pl
from jax.experimental.pallas import tpu as pltpu
from jax.sharding import Mesh
from jax.sharding import PartitionSpec as P

norm_eps = 1e-06
masked_score = -1e30
log2e = 1.4426950408889634
AXES = ("y", "zh", "x", "zl", "c")
SEQ = ("y", "zh", "x")
XY = ("y", "x")
TP = ("zl", "c")
SWAP = [(0, 1), (1, 0)]
BUILD_FLOPS = 100_000_000_000
VMEM_LIMIT = 40 * 1024 * 1024


def nt_dot(a, b):
    return lax.dot_general(a, b, (((1,), (1,)), ((), ())), preferred_element_type=jnp.float32)


def softmax_dot(scores, values, scale):
    top = jnp.max(scores, axis=-1, keepdims=True)
    lifted = jnp.exp2((scores - top) * (scale * log2e))
    total = jnp.sum(lifted, axis=-1, keepdims=True)
    out = jnp.dot(lifted.astype(jnp.bfloat16), values, preferred_element_type=jnp.float32)
    return (out / total).astype(jnp.bfloat16)


def params():
    return pltpu.CompilerParams(vmem_limit_bytes=VMEM_LIMIT)


def whole(array):
    return pl.BlockSpec(array.shape, lambda *_: (0,) * array.ndim)


def pick_kernel(zh_ref, x_ref, *refs):
    o_ref = refs[-1]
    ny, _, nx, height, lanes = x_ref.shape
    o_ref[:, :height] = x_ref[...].reshape(ny * nx, height, lanes)


def pick(zh, items, runs, earlier):
    ny, _, nx, height, lanes = items.shape
    return pl.pallas_call(
        pick_kernel,
        out_shape=jax.ShapeDtypeStruct((ny * nx, runs * height, lanes), items.dtype),
        grid_spec=pltpu.PrefetchScalarGridSpec(
            num_scalar_prefetch=1,
            grid=(2,),
            in_specs=[
                pl.BlockSpec(
                    (ny // 2, 1, nx, height, lanes), lambda i, zh_ref: (i, zh_ref[0], 0, 0, 0)
                )
            ]
            + [pl.BlockSpec(memory_space=pl.ANY)] * len(earlier),
            out_specs=pl.BlockSpec((ny // 2 * nx, height, lanes), lambda i, zh_ref: (i, 0, 0)),
        ),
        name="pick",
    )(zh, items, *earlier)


def build_kernel(zh_ref, x_ref, far_ref, o_ref):
    ny, _, nx, height, lanes = x_ref.shape
    o_ref[:, :height] = x_ref[...].reshape(ny * nx, height, lanes)
    o_ref[:, height:] = far_ref[...]


def build(zh, items, far):
    ny, _, nx, height, lanes = items.shape
    return pl.pallas_call(
        build_kernel,
        out_shape=jax.ShapeDtypeStruct((ny * nx, 2 * height, lanes), items.dtype),
        grid_spec=pltpu.PrefetchScalarGridSpec(
            num_scalar_prefetch=1,
            grid=(2,),
            in_specs=[
                pl.BlockSpec(
                    (ny // 2, 1, nx, height, lanes), lambda i, zh_ref: (i, zh_ref[0], 0, 0, 0)
                ),
                pl.BlockSpec((ny // 2 * nx, height, lanes), lambda i, zh_ref: (i, 0, 0)),
            ],
            out_specs=pl.BlockSpec((ny // 2 * nx, 2 * height, lanes), lambda i, zh_ref: (i, 0, 0)),
        ),
        cost_estimate=pl.CostEstimate(
            flops=BUILD_FLOPS, bytes_accessed=4 * items.size, transcendentals=0
        ),
        name="build",
    )(zh, items, far)


def place_kernel(x_ref, _, o_ref):
    o_ref[...] = x_ref[...]


def place(buffer, part, at):
    count, height, lanes = part.shape
    return pl.pallas_call(
        place_kernel,
        out_shape=jax.ShapeDtypeStruct(buffer.shape, buffer.dtype),
        grid=(2,),
        in_specs=[
            pl.BlockSpec((count // 2, height, lanes), lambda i: (i, 0, 0)),
            pl.BlockSpec(memory_space=pl.ANY),
        ],
        out_specs=pl.BlockSpec((count // 2, height, lanes), lambda i: (i, at, 0)),
        input_output_aliases={1: 0},
        name="place",
    )(part, buffer)


def take_kernel(x_ref, *refs):
    o_ref = refs[-1]
    o_ref[...] = x_ref[:, x_ref.shape[1] - o_ref.shape[1] :]


def take(buffer, first, height, earlier):
    count, _, lanes = buffer.shape
    return pl.pallas_call(
        take_kernel,
        out_shape=jax.ShapeDtypeStruct((count, height, lanes), buffer.dtype),
        grid=(2,),
        in_specs=[pl.BlockSpec((count // 2, first + height, lanes), lambda i: (i, 0, 0))]
        + [pl.BlockSpec(memory_space=pl.ANY)] * len(earlier),
        out_specs=pl.BlockSpec((count // 2, height, lanes), lambda i: (i, 0, 0)),
        name="take",
    )(buffer, *earlier)


def self_kernel(from_far, x_ref, *refs):
    o_ref = refs[-1]
    sources, local_len, head_size = o_ref.shape
    count = sources * local_len
    scale = head_size ** (-0.5) * log2e

    def slot(k):
        return x_ref[:, k * local_len : (k + 1) * local_len].reshape(count, head_size)

    ones = jnp.ones((count, head_size), jnp.bfloat16)
    keys = [slot(1), slot(4)]
    values = [jnp.concatenate([slot(k), ones], axis=1) for k in (2, 5)]
    queries = slot(3 * from_far)
    block = 2
    for at in range(0, sources, block):
        some = queries[at * local_len : (at + block) * local_len]
        scores = [nt_dot(some, k) for k in keys]
        top = jnp.maximum(*(jnp.max(s, axis=-1, keepdims=True) for s in scores))
        lifted = [jnp.exp2((s - top) * scale).astype(jnp.bfloat16) for s in scores]
        sums = [
            jnp.dot(l, v, preferred_element_type=jnp.float32) for l, v in zip(lifted, values)
        ]
        sums = sums[0] + sums[1]
        out = (sums[:, :head_size] / sums[:, head_size:]).astype(jnp.bfloat16)
        o_ref[at : at + block] = out.reshape(block, local_len, head_size)


def self_attention(packed, from_far, earlier, into=None):
    sources, total, head_size = packed.shape
    local_len = total // 6
    full_len = 2 * sources * local_len

    def kernel(*refs):
        self_kernel(from_far, *refs)

    room = local_len if into is None else into.shape[1]
    given = list(earlier) if into is None else [into] + list(earlier)
    return pl.pallas_call(
        kernel,
        out_shape=jax.ShapeDtypeStruct((sources, room, head_size), packed.dtype),
        grid=(1,),
        in_specs=[whole(packed)]
        + [pl.BlockSpec(memory_space=pl.ANY)] * len(given),
        out_specs=pl.BlockSpec(
            (sources, local_len, head_size), lambda i: (0, room // local_len - 1, 0)
        ),
        input_output_aliases={} if into is None else {1: 0},
        compiler_params=params(),
        cost_estimate=pl.CostEstimate(
            flops=2 * full_len * full_len * head_size,
            bytes_accessed=6 * full_len * head_size,
            transcendentals=full_len * full_len // 2,
        ),
        name="self_attention",
    )(packed, *given)


def project_kernel(w_first, got_ref, mine_ref, other_ref, part_ref, sent_ref):
    sources, taken, feats = mine_ref.shape
    head_size = part_ref.shape[-1] // 2
    for which, ref in enumerate((mine_ref, other_ref)):
        squares = jnp.zeros((taken, 1), jnp.float32)
        total = [jnp.zeros((taken, head_size), jnp.float32) for _ in range(2)]
        for s in range(sources):
            block = ref[s].astype(jnp.float32)
            squares += jnp.sum(block * block, axis=-1, keepdims=True)
            after = w_first + 2 * feats
            parts = got_ref[s, after : after + 16].astype(jnp.float32)
            gain = parts[0:1] + parts[1:2] + parts[2:3]
            scaled = (block * gain).astype(jnp.bfloat16)
            for k in range(2):
                at = w_first + k * feats
                total[k] += jnp.dot(
                    scaled, got_ref[s, at : at + feats], preferred_element_type=jnp.float32
                )
        both = jnp.concatenate(total, axis=1)
        part_ref[which * taken : (which + 1) * taken] = both
        sent_ref[which * taken : (which + 1) * taken] = both.astype(jnp.bfloat16)
        spread = jnp.broadcast_to(squares, (taken, 128)).T[:16]
        spread = jnp.concatenate([spread, jnp.zeros((16, 2 * head_size - taken))], axis=1)
        at = 2 * taken + 16 * which
        part_ref[at : at + 16] = spread
        for k in range(3):
            high = spread.astype(jnp.bfloat16)
            spread = spread - high.astype(jnp.float32)
            at = 2 * taken + 16 * (2 * k + which)
            sent_ref[at : at + 16] = high


def project(got, w_first, mine, other, head_size):
    sources, taken, feats = mine.shape

    def kernel(*refs):
        project_kernel(w_first, *refs)

    return pl.pallas_call(
        kernel,
        out_shape=(
            jax.ShapeDtypeStruct((2 * taken + 32, 2 * head_size), jnp.float32),
            jax.ShapeDtypeStruct((2 * taken + 96, 2 * head_size), jnp.bfloat16),
        ),
        compiler_params=params(),
        cost_estimate=pl.CostEstimate(
            flops=8 * taken * sources * feats * head_size,
            bytes_accessed=4 * got.size,
            transcendentals=0,
        ),
        name="project",
    )(got, mine, other)


def cross_kernel(full_width, *refs):
    q_refs, (part_a, part_b, allowed_ref, o_ref) = refs[:-4], refs[-4:]
    sources, local_len, head_size = q_refs[0].shape
    videos = len(q_refs)
    half = part_a.shape[0] // 2 - 16
    blocks, rows = 8, half // 4
    per = rows // videos
    inverse = []
    for which in range(2):
        at = 2 * half + 16 * which
        squares = part_a[at : at + 16, :half]
        for k in range(3):
            squares += part_b[at + 32 * k : at + 32 * k + 16, :half].astype(jnp.float32)
        squares = squares[:1]
        inv = lax.rsqrt(squares / full_width + norm_eps)
        inverse.append(jnp.broadcast_to(inv, (128, half)).T)
    kv = []
    for b in range(blocks):
        span = slice(b * rows, (b + 1) * rows)
        total = part_a[span] + part_b[span].astype(jnp.float32)
        at = (b % 4) * rows
        inv = inverse[b // 4][at : at + rows]
        kv.append(jnp.concatenate([total[:, :head_size] * inv, total[:, head_size:] * inv], axis=1))
    for v in range(videos):
        this = jnp.concatenate([blk[v * per : (v + 1) * per] for blk in kv], axis=0)
        this = this.astype(jnp.bfloat16)
        rows_of_v = slice(v * local_len, (v + 1) * local_len)
        for at in range(0, sources, 4):
            queries = q_refs[v][at : at + 4].reshape(4 * local_len, head_size)
            scores = nt_dot(queries, this[:, :head_size])
            scores = jnp.where(allowed_ref[v, 0:1] > 0, scores, masked_score)
            out = softmax_dot(scores, this[:, head_size:], head_size ** (-0.5))
            o_ref[at : at + 4, rows_of_v] = out.reshape(4, local_len, head_size)


def cross_attention(got, part, far_part, allowed, pair, local_len, room, full_width):
    sources, _, head_size = got.shape
    taken = pair * local_len
    count = sources * taken * allowed.shape[-1]

    def kernel(*refs):
        cross_kernel(full_width, *refs)

    return pl.pallas_call(
        kernel,
        out_shape=jax.ShapeDtypeStruct((sources, room, head_size), got.dtype),
        grid=(1,),
        in_specs=[
            pl.BlockSpec((sources, local_len, head_size), lambda i, at=at: (0, at, 0))
            for at in range(pair)
        ]
        + [whole(one) for one in (part, far_part, allowed)],
        out_specs=pl.BlockSpec((sources, taken, head_size), lambda i: (0, 0, 0)),
        compiler_params=params(),
        cost_estimate=pl.CostEstimate(
            flops=4 * count * head_size,
            bytes_accessed=4 * sources * taken * head_size,
            transcendentals=count,
        ),
        name="cross_attention",
    )(*[got] * pair, part, far_part, allowed)


def unpack_kernel(zh_ref, x_ref, self_ref, cross_ref):
    ny, pair, nx, local_len, head_size = self_ref.shape
    got = x_ref[...].reshape(ny, nx, 2 * pair * local_len, head_size)
    zh = zh_ref[0]
    for y in range(ny):
        for j in range(pair):
            cross_ref[y, j] = got[y, :, j * local_len : (j + 1) * local_len]
        self_ref[y, 1 - zh] = got[y, :, pair * local_len : (pair + 1) * local_len]
        self_ref[y, zh] = got[y, :, (pair + 1) * local_len :]


def unpack(zh, got, shape):
    ny, pair, nx, local_len, head_size = shape
    out = pl.BlockSpec((ny // 2,) + shape[1:], lambda i: (i, 0, 0, 0, 0))
    return pl.pallas_call(
        unpack_kernel,
        out_shape=(jax.ShapeDtypeStruct(shape, got.dtype),) * 2,
        grid=(2,),
        in_specs=[
            pl.BlockSpec(memory_space=pltpu.SMEM),
            pl.BlockSpec((ny // 2 * nx,) + got.shape[1:], lambda i: (i, 0, 0)),
        ],
        out_specs=(out, out),
        name="unpack",
    )(zh, got)


def hold_kernel(*refs):
    pass


def hold(value, earlier):
    return pl.pallas_call(
        hold_kernel,
        out_shape=jax.ShapeDtypeStruct(value.shape, value.dtype),
        in_specs=[pl.BlockSpec(memory_space=pl.ANY)] * (1 + len(earlier)),
        out_specs=pl.BlockSpec(memory_space=pl.ANY),
        input_output_aliases={0: 0},
        name="hold",
    )(value, *earlier)


def three_parts(values):
    high = lax.reduce_precision(values, 8, 7)
    rest = values - high
    middle = lax.reduce_precision(rest, 8, 7)
    return [p.astype(jnp.bfloat16) for p in (high, middle, rest - middle)]


def ahead(value, axis, step):
    return lax.ppermute(value, axis, [(i, (i + step) % 4) for i in range(4)])


def gather_ring(value, axis):
    return [value] + [ahead(value, axis, k) for k in (1, 3, 2)]


def ring_order(pieces):
    own, one, three, two = pieces
    return [own, one, two, three]


def body(video_qkv, cross_query, captions, caption_gain, key_value_weight, caption_lengths):
    videos, local_heads, local_len, slots, head_size = video_qkv.shape
    caption_len, feats = captions.shape[1:]
    ny, nx, nz = lax.axis_size("y"), lax.axis_size("x"), lax.axis_size("zl")
    pair, group, height = videos // ny, ny * nx, slots * local_len
    at_y, at_z, core = (lax.axis_index(a) for a in ("y", "zl", "c"))
    zh = lax.axis_index("zh").astype(jnp.int32).reshape(1)
    full_width = feats * group * 2

    items = video_qkv.transpose(0, 1, 3, 2, 4)
    items = items.reshape(ny, pair, nx, height, head_size)
    rows = ring_order(gather_ring(captions, "zl"))
    far = pick(1 - zh, items, 1, [])
    far = lax.ppermute(hold(far, rows[1:]), "zh", SWAP)
    rows = jnp.stack(rows).reshape(nz, ny, pair * caption_len, feats).transpose(1, 0, 2, 3)
    taken, asked = nz * pair * caption_len, pair * local_len
    rows = rows.reshape(ny, 1, taken, feats)
    queries = cross_query.reshape(ny, pair, nx, local_len, head_size).transpose(0, 2, 1, 3, 4)
    first = (at_z * 2 + core) * local_heads
    weights = lax.dynamic_slice_in_dim(key_value_weight, first, local_heads, axis=2)
    weights = weights.transpose(2, 1, 0, 3).reshape(1, nx, 2 * feats, head_size)
    gains = jnp.pad(jnp.stack(three_parts(caption_gain)), ((0, 13), (0, 0)))
    sent = jnp.concatenate(
        [
            queries.reshape(ny, nx, asked, head_size),
            jnp.broadcast_to(rows, (ny, nx, taken, feats)),
            jnp.broadcast_to(weights, (ny, nx, 2 * feats, head_size)),
            jnp.broadcast_to(gains, (ny, nx, 16, feats)),
        ],
        axis=2,
    ).reshape(group, asked + taken + 2 * feats + 16, feats)
    got = lax.all_to_all(sent, XY, split_axis=0, concat_axis=0, tiled=True)

    packed = hold(build(zh, items, far), [got])
    mine = take(got, asked, taken, [packed])
    other = lax.ppermute(mine, "c", SWAP)
    part, part_sent = project(got, asked + taken, mine, other, head_size)
    far_part = lax.ppermute(part_sent, "zh", SWAP)
    packed = lax.all_to_all(packed, XY, split_axis=0, concat_axis=0, tiled=True)

    far_out = self_attention(packed, 1, [part])
    far_out = lax.ppermute(far_out, "zh", SWAP)

    which, z, token = jnp.meshgrid(
        jnp.arange(2), jnp.arange(nz), jnp.arange(caption_len), indexing="ij"
    )
    cores = jnp.where(which == 0, core, 1 - core)
    positions = (((at_z + nz - z) % nz * 2 + cores) * caption_len + token).reshape(-1)
    lengths = lax.dynamic_slice_in_dim(caption_lengths, at_y * pair, pair)
    allowed = (positions[None, :] < lengths[:, None]).astype(jnp.float32)
    allowed = jnp.broadcast_to(allowed[:, None, :], (pair, 8, allowed.shape[-1]))
    outs = cross_attention(got, part, far_part, allowed, pair, local_len, 2 * asked, full_width)
    outs = self_attention(packed, 0, [], outs)
    outs = place(outs, far_out, pair)
    outs = lax.all_to_all(outs, XY, split_axis=0, concat_axis=0, tiled=True)
    self_out, cross_out = unpack(zh, outs, (ny, pair, nx, local_len, head_size))
    shape = (videos, local_heads, local_len, head_size)
    return (self_out.reshape(shape), cross_out.reshape(shape))


def solution(mesh):
    devices = mesh.devices.reshape(4, 2, 4, 4, 2)
    placed = (
        P(None, TP, SEQ, None, None),
        P(None, TP, SEQ, None),
        P(None, TP, SEQ),
        P(SEQ),
        P(SEQ, None, None, None),
        P(),
    )
    return jax.shard_map(
        body,
        mesh=Mesh(devices, AXES),
        in_specs=placed,
        out_specs=(P(None, TP, SEQ, None), P(None, TP, SEQ, None)),
        check_vma=False,
    )
```

```python
import jax
import jax.numpy as jnp
from jax import lax
from jax.experimental import pallas as pl
from jax.experimental.pallas import tpu as pltpu
from jax.sharding import Mesh
from jax.sharding import PartitionSpec as P

norm_eps = 1e-06
masked_score = -1e30
log2e = 1.4426950408889634
AXES = ("y", "zh", "x", "zl", "c")
SEQ = ("y", "zh", "x")
XY = ("y", "x")
TP = ("zl", "c")
SWAP = [(0, 1), (1, 0)]
BUILD_FLOPS = 100_000_000_000
VMEM_LIMIT = 40 * 1024 * 1024


def nt_dot(a, b):
    return lax.dot_general(a, b, (((1,), (1,)), ((), ())), preferred_element_type=jnp.float32)


def softmax_dot(scores, values, scale):
    top = jnp.max(scores, axis=-1, keepdims=True)
    lifted = jnp.exp2((scores - top) * (scale * log2e))
    total = jnp.sum(lifted, axis=-1, keepdims=True)
    out = jnp.dot(lifted.astype(jnp.bfloat16), values, preferred_element_type=jnp.float32)
    return (out / total).astype(jnp.bfloat16)


def params():
    return pltpu.CompilerParams(vmem_limit_bytes=VMEM_LIMIT)


def whole(array):
    return pl.BlockSpec(array.shape, lambda *_: (0,) * array.ndim)


def pick_kernel(zh_ref, x_ref, *refs):
    o_ref = refs[-1]
    ny, _, nx, height, lanes = x_ref.shape
    o_ref[:, :height] = x_ref[...].reshape(ny * nx, height, lanes)


def pick(zh, items, runs, earlier):
    ny, _, nx, height, lanes = items.shape
    return pl.pallas_call(
        pick_kernel,
        out_shape=jax.ShapeDtypeStruct((ny * nx, runs * height, lanes), items.dtype),
        grid_spec=pltpu.PrefetchScalarGridSpec(
            num_scalar_prefetch=1,
            grid=(2,),
            in_specs=[
                pl.BlockSpec(
                    (ny // 2, 1, nx, height, lanes), lambda i, zh_ref: (i, zh_ref[0], 0, 0, 0)
                )
            ]
            + [pl.BlockSpec(memory_space=pl.ANY)] * len(earlier),
            out_specs=pl.BlockSpec((ny // 2 * nx, height, lanes), lambda i, zh_ref: (i, 0, 0)),
        ),
        name="pick",
    )(zh, items, *earlier)


def build_kernel(zh_ref, x_ref, far_ref, o_ref):
    ny, _, nx, height, lanes = x_ref.shape
    o_ref[:, :height] = x_ref[...].reshape(ny * nx, height, lanes)
    o_ref[:, height:] = far_ref[...]


def build(zh, items, far):
    ny, _, nx, height, lanes = items.shape
    return pl.pallas_call(
        build_kernel,
        out_shape=jax.ShapeDtypeStruct((ny * nx, 2 * height, lanes), items.dtype),
        grid_spec=pltpu.PrefetchScalarGridSpec(
            num_scalar_prefetch=1,
            grid=(2,),
            in_specs=[
                pl.BlockSpec(
                    (ny // 2, 1, nx, height, lanes), lambda i, zh_ref: (i, zh_ref[0], 0, 0, 0)
                ),
                pl.BlockSpec((ny // 2 * nx, height, lanes), lambda i, zh_ref: (i, 0, 0)),
            ],
            out_specs=pl.BlockSpec((ny // 2 * nx, 2 * height, lanes), lambda i, zh_ref: (i, 0, 0)),
        ),
        cost_estimate=pl.CostEstimate(
            flops=BUILD_FLOPS, bytes_accessed=4 * items.size, transcendentals=0
        ),
        name="build",
    )(zh, items, far)


def take_kernel(x_ref, *refs):
    o_ref = refs[-1]
    o_ref[...] = x_ref[:, x_ref.shape[1] - o_ref.shape[1] :]


def take(buffer, first, height, earlier):
    count, _, lanes = buffer.shape
    return pl.pallas_call(
        take_kernel,
        out_shape=jax.ShapeDtypeStruct((count, height, lanes), buffer.dtype),
        grid=(2,),
        in_specs=[pl.BlockSpec((count // 2, first + height, lanes), lambda i: (i, 0, 0))]
        + [pl.BlockSpec(memory_space=pl.ANY)] * len(earlier),
        out_specs=pl.BlockSpec((count // 2, height, lanes), lambda i: (i, 0, 0)),
        name="take",
    )(buffer, *earlier)


def self_kernel(from_far, x_ref, *refs):
    o_ref = refs[-1]
    sources, local_len, head_size = o_ref.shape
    count = sources * local_len
    scale = head_size ** (-0.5) * log2e

    def slot(k):
        return x_ref[:, k * local_len : (k + 1) * local_len].reshape(count, head_size)

    ones = jnp.ones((count, head_size), jnp.bfloat16)
    keys = [slot(1), slot(4)]
    values = [jnp.concatenate([slot(k), ones], axis=1) for k in (2, 5)]
    queries = slot(3 * from_far)
    block = 2
    for at in range(0, sources, block):
        some = queries[at * local_len : (at + block) * local_len]
        scores = [nt_dot(some, k) for k in keys]
        top = jnp.maximum(*(jnp.max(s, axis=-1, keepdims=True) for s in scores))
        lifted = [jnp.exp2((s - top) * scale).astype(jnp.bfloat16) for s in scores]
        sums = [
            jnp.dot(l, v, preferred_element_type=jnp.float32) for l, v in zip(lifted, values)
        ]
        sums = sums[0] + sums[1]
        out = (sums[:, :head_size] / sums[:, head_size:]).astype(jnp.bfloat16)
        o_ref[at : at + block] = out.reshape(block, local_len, head_size)


def self_attention(packed, from_far, earlier, into=None):
    sources, total, head_size = packed.shape
    local_len = total // 6
    full_len = 2 * sources * local_len

    def kernel(*refs):
        self_kernel(from_far, *refs)

    room = local_len if into is None else into.shape[1]
    given = list(earlier) if into is None else [into] + list(earlier)
    return pl.pallas_call(
        kernel,
        out_shape=jax.ShapeDtypeStruct((sources, room, head_size), packed.dtype),
        grid=(1,),
        in_specs=[whole(packed)]
        + [pl.BlockSpec(memory_space=pl.ANY)] * len(given),
        out_specs=pl.BlockSpec(
            (sources, local_len, head_size), lambda i: (0, room // local_len - 1, 0)
        ),
        input_output_aliases={} if into is None else {1: 0},
        compiler_params=params(),
        cost_estimate=pl.CostEstimate(
            flops=2 * full_len * full_len * head_size,
            bytes_accessed=6 * full_len * head_size,
            transcendentals=full_len * full_len // 2,
        ),
        name="self_attention",
    )(packed, *given)


def project_kernel(w_first, got_ref, mine_ref, other_ref, part_ref, sent_ref):
    sources, taken, feats = mine_ref.shape
    head_size = part_ref.shape[-1] // 2
    for which, ref in enumerate((mine_ref, other_ref)):
        squares = jnp.zeros((taken, 1), jnp.float32)
        total = [jnp.zeros((taken, head_size), jnp.float32) for _ in range(2)]
        for s in range(sources):
            block = ref[s].astype(jnp.float32)
            squares += jnp.sum(block * block, axis=-1, keepdims=True)
            after = w_first + 2 * feats
            parts = got_ref[s, after : after + 16].astype(jnp.float32)
            gain = parts[0:1] + parts[1:2] + parts[2:3]
            scaled = (block * gain).astype(jnp.bfloat16)
            for k in range(2):
                at = w_first + k * feats
                total[k] += jnp.dot(
                    scaled, got_ref[s, at : at + feats], preferred_element_type=jnp.float32
                )
        both = jnp.concatenate(total, axis=1)
        part_ref[which * taken : (which + 1) * taken] = both
        sent_ref[which * taken : (which + 1) * taken] = both.astype(jnp.bfloat16)
        spread = jnp.broadcast_to(squares, (taken, 128)).T[:16]
        spread = jnp.concatenate([spread, jnp.zeros((16, 2 * head_size - taken))], axis=1)
        at = 2 * taken + 16 * which
        part_ref[at : at + 16] = spread
        for k in range(3):
            high = spread.astype(jnp.bfloat16)
            spread = spread - high.astype(jnp.float32)
            at = 2 * taken + 16 * (2 * k + which)
            sent_ref[at : at + 16] = high


def project(got, w_first, mine, other, head_size):
    sources, taken, feats = mine.shape

    def kernel(*refs):
        project_kernel(w_first, *refs)

    return pl.pallas_call(
        kernel,
        out_shape=(
            jax.ShapeDtypeStruct((2 * taken + 32, 2 * head_size), jnp.float32),
            jax.ShapeDtypeStruct((2 * taken + 96, 2 * head_size), jnp.bfloat16),
        ),
        compiler_params=params(),
        cost_estimate=pl.CostEstimate(
            flops=8 * taken * sources * feats * head_size,
            bytes_accessed=4 * got.size,
            transcendentals=0,
        ),
        name="project",
    )(got, mine, other)


def cross_kernel(full_width, *refs):
    q_refs, (part_a, part_b, allowed_ref, o_ref) = refs[:-4], refs[-4:]
    sources, local_len, head_size = q_refs[0].shape
    videos = len(q_refs)
    half = part_a.shape[0] // 2 - 16
    blocks, rows = 8, half // 4
    per = rows // videos
    inverse = []
    for which in range(2):
        at = 2 * half + 16 * which
        squares = part_a[at : at + 16, :half]
        for k in range(3):
            squares += part_b[at + 32 * k : at + 32 * k + 16, :half].astype(jnp.float32)
        squares = squares[:1]
        inv = lax.rsqrt(squares / full_width + norm_eps)
        inverse.append(jnp.broadcast_to(inv, (128, half)).T)
    kv = []
    for b in range(blocks):
        span = slice(b * rows, (b + 1) * rows)
        total = part_a[span] + part_b[span].astype(jnp.float32)
        at = (b % 4) * rows
        inv = inverse[b // 4][at : at + rows]
        kv.append(jnp.concatenate([total[:, :head_size] * inv, total[:, head_size:] * inv], axis=1))
    for v in range(videos):
        this = jnp.concatenate([blk[v * per : (v + 1) * per] for blk in kv], axis=0)
        this = this.astype(jnp.bfloat16)
        rows_of_v = slice(v * local_len, (v + 1) * local_len)
        for at in range(0, sources, 4):
            queries = q_refs[v][at : at + 4].reshape(4 * local_len, head_size)
            scores = nt_dot(queries, this[:, :head_size])
            scores = jnp.where(allowed_ref[v, 0:1] > 0, scores, masked_score)
            out = softmax_dot(scores, this[:, head_size:], head_size ** (-0.5))
            o_ref[at : at + 4, rows_of_v] = out.reshape(4, local_len, head_size)


def cross_attention(got, part, far_part, allowed, pair, local_len, room, full_width):
    sources, _, head_size = got.shape
    taken = pair * local_len
    count = sources * taken * allowed.shape[-1]

    def kernel(*refs):
        cross_kernel(full_width, *refs)

    return pl.pallas_call(
        kernel,
        out_shape=jax.ShapeDtypeStruct((sources, room, head_size), got.dtype),
        grid=(1,),
        in_specs=[
            pl.BlockSpec((sources, local_len, head_size), lambda i, at=at: (0, at, 0))
            for at in range(pair)
        ]
        + [whole(one) for one in (part, far_part, allowed)],
        out_specs=pl.BlockSpec((sources, taken, head_size), lambda i: (0, 0, 0)),
        compiler_params=params(),
        cost_estimate=pl.CostEstimate(
            flops=4 * count * head_size,
            bytes_accessed=4 * sources * taken * head_size,
            transcendentals=count,
        ),
        name="cross_attention",
    )(*[got] * pair, part, far_part, allowed)


def unpack_kernel(zh_ref, x_ref, self_ref, cross_ref):
    ny, pair, nx, local_len, head_size = self_ref.shape
    got = x_ref[...].reshape(ny, nx, 2 * pair * local_len, head_size)
    zh = zh_ref[0]
    for y in range(ny):
        for j in range(pair):
            cross_ref[y, j] = got[y, :, j * local_len : (j + 1) * local_len]
        self_ref[y, 1 - zh] = got[y, :, pair * local_len : (pair + 1) * local_len]
        self_ref[y, zh] = got[y, :, (pair + 1) * local_len :]


def unpack(zh, got, shape):
    ny, pair, nx, local_len, head_size = shape
    out = pl.BlockSpec((ny // 2,) + shape[1:], lambda i: (i, 0, 0, 0, 0))
    return pl.pallas_call(
        unpack_kernel,
        out_shape=(jax.ShapeDtypeStruct(shape, got.dtype),) * 2,
        grid=(2,),
        in_specs=[
            pl.BlockSpec(memory_space=pltpu.SMEM),
            pl.BlockSpec((ny // 2 * nx,) + got.shape[1:], lambda i: (i, 0, 0)),
        ],
        out_specs=(out, out),
        name="unpack",
    )(zh, got)


def hold_kernel(*refs):
    pass


def hold(value, earlier):
    return pl.pallas_call(
        hold_kernel,
        out_shape=jax.ShapeDtypeStruct(value.shape, value.dtype),
        in_specs=[pl.BlockSpec(memory_space=pl.ANY)] * (1 + len(earlier)),
        out_specs=pl.BlockSpec(memory_space=pl.ANY),
        input_output_aliases={0: 0},
        name="hold",
    )(value, *earlier)


def three_parts(values):
    high = lax.reduce_precision(values, 8, 7)
    rest = values - high
    middle = lax.reduce_precision(rest, 8, 7)
    return [p.astype(jnp.bfloat16) for p in (high, middle, rest - middle)]


def ahead(value, axis, step):
    return lax.ppermute(value, axis, [(i, (i + step) % 4) for i in range(4)])


def gather_ring(value, axis):
    return [value] + [ahead(value, axis, k) for k in (1, 3, 2)]


def ring_order(pieces):
    own, one, three, two = pieces
    return [own, one, two, three]


def body(video_qkv, cross_query, captions, caption_gain, key_value_weight, caption_lengths):
    videos, local_heads, local_len, slots, head_size = video_qkv.shape
    caption_len, feats = captions.shape[1:]
    ny, nx, nz = lax.axis_size("y"), lax.axis_size("x"), lax.axis_size("zl")
    pair, group, height = videos // ny, ny * nx, slots * local_len
    at_y, at_z, core = (lax.axis_index(a) for a in ("y", "zl", "c"))
    zh = lax.axis_index("zh").astype(jnp.int32).reshape(1)
    full_width = feats * group * 2

    items = video_qkv.transpose(0, 1, 3, 2, 4)
    items = items.reshape(ny, pair, nx, height, head_size)
    rows = ring_order(gather_ring(captions, "zl"))
    far = pick(1 - zh, items, 1, [])
    far = lax.ppermute(hold(far, rows[1:]), "zh", SWAP)
    rows = jnp.stack(rows).reshape(nz, ny, pair * caption_len, feats).transpose(1, 0, 2, 3)
    taken, asked = nz * pair * caption_len, pair * local_len
    rows = rows.reshape(ny, 1, taken, feats)
    queries = cross_query.reshape(ny, pair, nx, local_len, head_size).transpose(0, 2, 1, 3, 4)
    first = (at_z * 2 + core) * local_heads
    weights = lax.dynamic_slice_in_dim(key_value_weight, first, local_heads, axis=2)
    weights = weights.transpose(2, 1, 0, 3).reshape(1, nx, 2 * feats, head_size)
    gains = jnp.pad(jnp.stack(three_parts(caption_gain)), ((0, 13), (0, 0)))
    sent = jnp.concatenate(
        [
            queries.reshape(ny, nx, asked, head_size),
            jnp.broadcast_to(rows, (ny, nx, taken, feats)),
            jnp.broadcast_to(weights, (ny, nx, 2 * feats, head_size)),
            jnp.broadcast_to(gains, (ny, nx, 16, feats)),
        ],
        axis=2,
    ).reshape(group, asked + taken + 2 * feats + 16, feats)
    got = lax.all_to_all(sent, XY, split_axis=0, concat_axis=0, tiled=True)

    packed = hold(build(zh, items, far), [got])
    mine = take(got, asked, taken, [packed])
    other = lax.ppermute(mine, "c", SWAP)
    part, part_sent = project(got, asked + taken, mine, other, head_size)
    far_part = lax.ppermute(part_sent, "zh", SWAP)
    packed = lax.all_to_all(packed, XY, split_axis=0, concat_axis=0, tiled=True)

    far_out = self_attention(packed, 1, [part])
    far_out = lax.ppermute(far_out, "zh", SWAP)

    which, z, token = jnp.meshgrid(
        jnp.arange(2), jnp.arange(nz), jnp.arange(caption_len), indexing="ij"
    )
    cores = jnp.where(which == 0, core, 1 - core)
    positions = (((at_z + nz - z) % nz * 2 + cores) * caption_len + token).reshape(-1)
    lengths = lax.dynamic_slice_in_dim(caption_lengths, at_y * pair, pair)
    allowed = (positions[None, :] < lengths[:, None]).astype(jnp.float32)
    allowed = jnp.broadcast_to(allowed[:, None, :], (pair, 8, allowed.shape[-1]))
    crossed = cross_attention(got, part, far_part, allowed, pair, local_len, asked, full_width)
    near_out = self_attention(packed, 0, [crossed])
    outs = jnp.concatenate([crossed, far_out, near_out], axis=1)
    outs = lax.all_to_all(outs, XY, split_axis=0, concat_axis=0, tiled=True)
    self_out, cross_out = unpack(zh, outs, (ny, pair, nx, local_len, head_size))
    shape = (videos, local_heads, local_len, head_size)
    return (self_out.reshape(shape), cross_out.reshape(shape))


def solution(mesh):
    devices = mesh.devices.reshape(4, 2, 4, 4, 2)
    placed = (
        P(None, TP, SEQ, None, None),
        P(None, TP, SEQ, None),
        P(None, TP, SEQ),
        P(SEQ),
        P(SEQ, None, None, None),
        P(),
    )
    return jax.shard_map(
        body,
        mesh=Mesh(devices, AXES),
        in_specs=placed,
        out_specs=(P(None, TP, SEQ, None), P(None, TP, SEQ, None)),
        check_vma=False,
    )
```

```python
import jax
import jax.numpy as jnp
from jax import lax
from jax.experimental import pallas as pl
from jax.experimental.pallas import tpu as pltpu
from jax.sharding import Mesh
from jax.sharding import PartitionSpec as P

norm_eps = 1e-06
masked_score = -1e30
log2e = 1.4426950408889634
AXES = ("y", "zh", "x", "zl", "c")
SEQ = ("y", "zh", "x")
XY = ("y", "x")
TP = ("zl", "c")
SWAP = [(0, 1), (1, 0)]
BUILD_FLOPS = 100_000_000_000
VMEM_LIMIT = 40 * 1024 * 1024


def nt_dot(a, b):
    return lax.dot_general(a, b, (((1,), (1,)), ((), ())), preferred_element_type=jnp.float32)


def softmax_dot(scores, values, scale):
    top = jnp.max(scores, axis=-1, keepdims=True)
    lifted = jnp.exp2((scores - top) * (scale * log2e))
    total = jnp.sum(lifted, axis=-1, keepdims=True)
    out = jnp.dot(lifted.astype(jnp.bfloat16), values, preferred_element_type=jnp.float32)
    return (out / total).astype(jnp.bfloat16)


def params():
    return pltpu.CompilerParams(vmem_limit_bytes=VMEM_LIMIT)


def whole(array):
    return pl.BlockSpec(array.shape, lambda *_: (0,) * array.ndim)


def pick_kernel(zh_ref, x_ref, *refs):
    o_ref = refs[-1]
    ny, _, nx, height, lanes = x_ref.shape
    o_ref[:, :height] = x_ref[...].reshape(ny * nx, height, lanes)


def pick(zh, items, runs, earlier):
    ny, _, nx, height, lanes = items.shape
    return pl.pallas_call(
        pick_kernel,
        out_shape=jax.ShapeDtypeStruct((ny * nx, runs * height, lanes), items.dtype),
        grid_spec=pltpu.PrefetchScalarGridSpec(
            num_scalar_prefetch=1,
            grid=(2,),
            in_specs=[
                pl.BlockSpec(
                    (ny // 2, 1, nx, height, lanes), lambda i, zh_ref: (i, zh_ref[0], 0, 0, 0)
                )
            ]
            + [pl.BlockSpec(memory_space=pl.ANY)] * len(earlier),
            out_specs=pl.BlockSpec((ny // 2 * nx, height, lanes), lambda i, zh_ref: (i, 0, 0)),
        ),
        name="pick",
    )(zh, items, *earlier)


def build_kernel(zh_ref, x_ref, far_ref, o_ref):
    ny, _, nx, height, lanes = x_ref.shape
    o_ref[:, :height] = x_ref[...].reshape(ny * nx, height, lanes)
    o_ref[:, height:] = far_ref[...]


def build(zh, items, far):
    ny, _, nx, height, lanes = items.shape
    return pl.pallas_call(
        build_kernel,
        out_shape=jax.ShapeDtypeStruct((ny * nx, 2 * height, lanes), items.dtype),
        grid_spec=pltpu.PrefetchScalarGridSpec(
            num_scalar_prefetch=1,
            grid=(2,),
            in_specs=[
                pl.BlockSpec(
                    (ny // 2, 1, nx, height, lanes), lambda i, zh_ref: (i, zh_ref[0], 0, 0, 0)
                ),
                pl.BlockSpec((ny // 2 * nx, height, lanes), lambda i, zh_ref: (i, 0, 0)),
            ],
            out_specs=pl.BlockSpec((ny // 2 * nx, 2 * height, lanes), lambda i, zh_ref: (i, 0, 0)),
        ),
        cost_estimate=pl.CostEstimate(
            flops=BUILD_FLOPS, bytes_accessed=4 * items.size, transcendentals=0
        ),
        name="build",
    )(zh, items, far)


def take_kernel(x_ref, *refs):
    o_ref = refs[-1]
    o_ref[...] = x_ref[:, x_ref.shape[1] - o_ref.shape[1] :]


def take(buffer, first, height, earlier):
    count, _, lanes = buffer.shape
    return pl.pallas_call(
        take_kernel,
        out_shape=jax.ShapeDtypeStruct((count, height, lanes), buffer.dtype),
        grid=(2,),
        in_specs=[pl.BlockSpec((count // 2, first + height, lanes), lambda i: (i, 0, 0))]
        + [pl.BlockSpec(memory_space=pl.ANY)] * len(earlier),
        out_specs=pl.BlockSpec((count // 2, height, lanes), lambda i: (i, 0, 0)),
        name="take",
    )(buffer, *earlier)


def self_kernel(*refs):
    o_ref = refs[-1]
    sources, local_len, head_size = o_ref.shape
    count = sources * local_len
    scale = head_size ** (-0.5) * log2e

    queries, *rest = (r[...].reshape(count, head_size) for r in refs[:5])
    keys, given = rest[:2], rest[2:]
    ones = jnp.ones((count, head_size), jnp.bfloat16)
    values = [jnp.concatenate([v, ones], axis=1) for v in given]
    block = 2
    for at in range(0, sources, block):
        some = queries[at * local_len : (at + block) * local_len]
        scores = [nt_dot(some, k) for k in keys]
        top = jnp.maximum(*(jnp.max(s, axis=-1, keepdims=True) for s in scores))
        lifted = [jnp.exp2((s - top) * scale).astype(jnp.bfloat16) for s in scores]
        sums = [
            jnp.dot(l, v, preferred_element_type=jnp.float32) for l, v in zip(lifted, values)
        ]
        sums = sums[0] + sums[1]
        out = (sums[:, :head_size] / sums[:, head_size:]).astype(jnp.bfloat16)
        o_ref[at : at + block] = out.reshape(block, local_len, head_size)


def self_attention(packed, from_far, earlier, into=None):
    sources, total, head_size = packed.shape
    local_len = total // 6
    full_len = 2 * sources * local_len

    def kernel(*refs):
        self_kernel(*refs)

    room = local_len if into is None else into.shape[1]
    given = list(earlier) if into is None else [into] + list(earlier)
    return pl.pallas_call(
        kernel,
        out_shape=jax.ShapeDtypeStruct((sources, room, head_size), packed.dtype),
        grid=(1,),
        in_specs=[
            pl.BlockSpec((sources, local_len, head_size), lambda i, k=k: (0, k, 0))
            for k in (3 * from_far, 1, 4, 2, 5)
        ]
        + [pl.BlockSpec(memory_space=pl.ANY)] * len(given),
        out_specs=pl.BlockSpec(
            (sources, local_len, head_size), lambda i: (0, room // local_len - 1, 0)
        ),
        input_output_aliases={} if into is None else {5: 0},
        compiler_params=params(),
        cost_estimate=pl.CostEstimate(
            flops=2 * full_len * full_len * head_size,
            bytes_accessed=6 * full_len * head_size,
            transcendentals=full_len * full_len // 2,
        ),
        name="self_attention",
    )(*[packed] * 5, *given)


def project_kernel(w_first, got_ref, mine_ref, other_ref, part_ref, sent_ref):
    sources, taken, feats = mine_ref.shape
    head_size = part_ref.shape[-1] // 2
    for which, ref in enumerate((mine_ref, other_ref)):
        squares = jnp.zeros((taken, 1), jnp.float32)
        total = [jnp.zeros((taken, head_size), jnp.float32) for _ in range(2)]
        for s in range(sources):
            block = ref[s].astype(jnp.float32)
            squares += jnp.sum(block * block, axis=-1, keepdims=True)
            after = w_first + 2 * feats
            parts = got_ref[s, after : after + 16].astype(jnp.float32)
            gain = parts[0:1] + parts[1:2] + parts[2:3]
            scaled = (block * gain).astype(jnp.bfloat16)
            for k in range(2):
                at = w_first + k * feats
                total[k] += jnp.dot(
                    scaled, got_ref[s, at : at + feats], preferred_element_type=jnp.float32
                )
        both = jnp.concatenate(total, axis=1)
        part_ref[which * taken : (which + 1) * taken] = both
        sent_ref[which * taken : (which + 1) * taken] = both.astype(jnp.bfloat16)
        spread = jnp.broadcast_to(squares, (taken, 128)).T[:16]
        spread = jnp.concatenate([spread, jnp.zeros((16, 2 * head_size - taken))], axis=1)
        at = 2 * taken + 16 * which
        part_ref[at : at + 16] = spread
        for k in range(3):
            high = spread.astype(jnp.bfloat16)
            spread = spread - high.astype(jnp.float32)
            at = 2 * taken + 16 * (2 * k + which)
            sent_ref[at : at + 16] = high


def project(got, w_first, mine, other, head_size):
    sources, taken, feats = mine.shape

    def kernel(*refs):
        project_kernel(w_first, *refs)

    return pl.pallas_call(
        kernel,
        out_shape=(
            jax.ShapeDtypeStruct((2 * taken + 32, 2 * head_size), jnp.float32),
            jax.ShapeDtypeStruct((2 * taken + 96, 2 * head_size), jnp.bfloat16),
        ),
        compiler_params=params(),
        cost_estimate=pl.CostEstimate(
            flops=8 * taken * sources * feats * head_size,
            bytes_accessed=4 * got.size,
            transcendentals=0,
        ),
        name="project",
    )(got, mine, other)


def cross_kernel(full_width, *refs):
    q_refs, (part_a, part_b, allowed_ref, o_ref) = refs[:-4], refs[-4:]
    sources, local_len, head_size = q_refs[0].shape
    videos = len(q_refs)
    half = part_a.shape[0] // 2 - 16
    blocks, rows = 8, half // 4
    per = rows // videos
    inverse = []
    for which in range(2):
        at = 2 * half + 16 * which
        squares = part_a[at : at + 16, :half]
        for k in range(3):
            squares += part_b[at + 32 * k : at + 32 * k + 16, :half].astype(jnp.float32)
        squares = squares[:1]
        inv = lax.rsqrt(squares / full_width + norm_eps)
        inverse.append(jnp.broadcast_to(inv, (128, half)).T)
    kv = []
    for b in range(blocks):
        span = slice(b * rows, (b + 1) * rows)
        total = part_a[span] + part_b[span].astype(jnp.float32)
        at = (b % 4) * rows
        inv = inverse[b // 4][at : at + rows]
        kv.append(jnp.concatenate([total[:, :head_size] * inv, total[:, head_size:] * inv], axis=1))
    for v in range(videos):
        this = jnp.concatenate([blk[v * per : (v + 1) * per] for blk in kv], axis=0)
        this = this.astype(jnp.bfloat16)
        rows_of_v = slice(v * local_len, (v + 1) * local_len)
        for at in range(0, sources, 4):
            queries = q_refs[v][at : at + 4].reshape(4 * local_len, head_size)
            scores = nt_dot(queries, this[:, :head_size])
            scores = jnp.where(allowed_ref[v, 0:1] > 0, scores, masked_score)
            out = softmax_dot(scores, this[:, head_size:], head_size ** (-0.5))
            o_ref[at : at + 4, rows_of_v] = out.reshape(4, local_len, head_size)


def cross_attention(got, part, far_part, allowed, pair, local_len, room, full_width):
    sources, _, head_size = got.shape
    taken = pair * local_len
    count = sources * taken * allowed.shape[-1]

    def kernel(*refs):
        cross_kernel(full_width, *refs)

    return pl.pallas_call(
        kernel,
        out_shape=jax.ShapeDtypeStruct((sources, room, head_size), got.dtype),
        grid=(1,),
        in_specs=[
            pl.BlockSpec((sources, local_len, head_size), lambda i, at=at: (0, at, 0))
            for at in range(pair)
        ]
        + [whole(one) for one in (part, far_part, allowed)],
        out_specs=pl.BlockSpec((sources, taken, head_size), lambda i: (0, 0, 0)),
        compiler_params=params(),
        cost_estimate=pl.CostEstimate(
            flops=4 * count * head_size,
            bytes_accessed=4 * sources * taken * head_size,
            transcendentals=count,
        ),
        name="cross_attention",
    )(*[got] * pair, part, far_part, allowed)


def unpack_kernel(zh_ref, x_ref, self_ref, cross_ref):
    ny, pair, nx, local_len, head_size = self_ref.shape
    got = x_ref[...].reshape(ny, nx, 2 * pair * local_len, head_size)
    zh = zh_ref[0]
    for y in range(ny):
        for j in range(pair):
            cross_ref[y, j] = got[y, :, j * local_len : (j + 1) * local_len]
        self_ref[y, 1 - zh] = got[y, :, pair * local_len : (pair + 1) * local_len]
        self_ref[y, zh] = got[y, :, (pair + 1) * local_len :]


def unpack(zh, got, shape):
    ny, pair, nx, local_len, head_size = shape
    out = pl.BlockSpec((ny // 2,) + shape[1:], lambda i: (i, 0, 0, 0, 0))
    return pl.pallas_call(
        unpack_kernel,
        out_shape=(jax.ShapeDtypeStruct(shape, got.dtype),) * 2,
        grid=(2,),
        in_specs=[
            pl.BlockSpec(memory_space=pltpu.SMEM),
            pl.BlockSpec((ny // 2 * nx,) + got.shape[1:], lambda i: (i, 0, 0)),
        ],
        out_specs=(out, out),
        name="unpack",
    )(zh, got)


def hold_kernel(*refs):
    pass


def hold(value, earlier):
    return pl.pallas_call(
        hold_kernel,
        out_shape=jax.ShapeDtypeStruct(value.shape, value.dtype),
        in_specs=[pl.BlockSpec(memory_space=pl.ANY)] * (1 + len(earlier)),
        out_specs=pl.BlockSpec(memory_space=pl.ANY),
        input_output_aliases={0: 0},
        name="hold",
    )(value, *earlier)


def three_parts(values):
    high = lax.reduce_precision(values, 8, 7)
    rest = values - high
    middle = lax.reduce_precision(rest, 8, 7)
    return [p.astype(jnp.bfloat16) for p in (high, middle, rest - middle)]


def ahead(value, axis, step):
    return lax.ppermute(value, axis, [(i, (i + step) % 4) for i in range(4)])


def gather_ring(value, axis):
    return [value] + [ahead(value, axis, k) for k in (1, 3, 2)]


def ring_order(pieces):
    own, one, three, two = pieces
    return [own, one, two, three]


def body(video_qkv, cross_query, captions, caption_gain, key_value_weight, caption_lengths):
    videos, local_heads, local_len, slots, head_size = video_qkv.shape
    caption_len, feats = captions.shape[1:]
    ny, nx, nz = lax.axis_size("y"), lax.axis_size("x"), lax.axis_size("zl")
    pair, group, height = videos // ny, ny * nx, slots * local_len
    at_y, at_z, core = (lax.axis_index(a) for a in ("y", "zl", "c"))
    zh = lax.axis_index("zh").astype(jnp.int32).reshape(1)
    full_width = feats * group * 2

    items = video_qkv.transpose(0, 1, 3, 2, 4)
    items = items.reshape(ny, pair, nx, height, head_size)
    rows = ring_order(gather_ring(captions, "zl"))
    far = pick(1 - zh, items, 1, [])
    far = lax.ppermute(hold(far, rows[1:]), "zh", SWAP)
    rows = jnp.stack(rows).reshape(nz, ny, pair * caption_len, feats).transpose(1, 0, 2, 3)
    taken, asked = nz * pair * caption_len, pair * local_len
    rows = rows.reshape(ny, 1, taken, feats)
    queries = cross_query.reshape(ny, pair, nx, local_len, head_size).transpose(0, 2, 1, 3, 4)
    first = (at_z * 2 + core) * local_heads
    weights = lax.dynamic_slice_in_dim(key_value_weight, first, local_heads, axis=2)
    weights = weights.transpose(2, 1, 0, 3).reshape(1, nx, 2 * feats, head_size)
    gains = jnp.pad(jnp.stack(three_parts(caption_gain)), ((0, 13), (0, 0)))
    sent = jnp.concatenate(
        [
            queries.reshape(ny, nx, asked, head_size),
            jnp.broadcast_to(rows, (ny, nx, taken, feats)),
            jnp.broadcast_to(weights, (ny, nx, 2 * feats, head_size)),
            jnp.broadcast_to(gains, (ny, nx, 16, feats)),
        ],
        axis=2,
    ).reshape(group, asked + taken + 2 * feats + 16, feats)
    got = lax.all_to_all(sent, XY, split_axis=0, concat_axis=0, tiled=True)

    packed = hold(build(zh, items, far), [got])
    mine = take(got, asked, taken, [packed])
    other = lax.ppermute(mine, "c", SWAP)
    part, part_sent = project(got, asked + taken, mine, other, head_size)
    far_part = lax.ppermute(part_sent, "zh", SWAP)
    packed = lax.all_to_all(packed, XY, split_axis=0, concat_axis=0, tiled=True)

    far_out = self_attention(packed, 1, [part])
    far_out = lax.ppermute(far_out, "zh", SWAP)

    which, z, token = jnp.meshgrid(
        jnp.arange(2), jnp.arange(nz), jnp.arange(caption_len), indexing="ij"
    )
    cores = jnp.where(which == 0, core, 1 - core)
    positions = (((at_z + nz - z) % nz * 2 + cores) * caption_len + token).reshape(-1)
    lengths = lax.dynamic_slice_in_dim(caption_lengths, at_y * pair, pair)
    allowed = (positions[None, :] < lengths[:, None]).astype(jnp.float32)
    allowed = jnp.broadcast_to(allowed[:, None, :], (pair, 8, allowed.shape[-1]))
    crossed = cross_attention(got, part, far_part, allowed, pair, local_len, asked, full_width)
    near_out = self_attention(packed, 0, [crossed])
    outs = jnp.concatenate([crossed, far_out, near_out], axis=1)
    outs = lax.all_to_all(outs, XY, split_axis=0, concat_axis=0, tiled=True)
    self_out, cross_out = unpack(zh, outs, (ny, pair, nx, local_len, head_size))
    shape = (videos, local_heads, local_len, head_size)
    return (self_out.reshape(shape), cross_out.reshape(shape))


def solution(mesh):
    devices = mesh.devices.reshape(4, 2, 4, 4, 2)
    placed = (
        P(None, TP, SEQ, None, None),
        P(None, TP, SEQ, None),
        P(None, TP, SEQ),
        P(SEQ),
        P(SEQ, None, None, None),
        P(),
    )
    return jax.shard_map(
        body,
        mesh=Mesh(devices, AXES),
        in_specs=placed,
        out_specs=(P(None, TP, SEQ, None), P(None, TP, SEQ, None)),
        check_vma=False,
    )
```
